32 devices in a mesh: ctx: 4 (over y, core), head: 2 (over x), seq: 4 (over z).
Axes of the slice: x: 2, y: 2, z: 4, core: 2. Of those that a mesh axis runs over, the one named last changes fastest.
Arguments:
- queries: bfloat16 [2048, 64, 128], P(('seq', 'ctx'), 'head'), parts along dimension 0, may hold values from -100 to 100
- keys: bfloat16 [2048, 4, 128], P(('seq', 'ctx'), 'head'), parts along dimension 0, may hold values from -8 to 8
- values: bfloat16 [2048, 4, 128], P(('seq', 'ctx'), 'head'), parts along dimension 0, may hold values from -6 to 6
Outputs:
- attended: bfloat16 [2048, 64, 128], P(('seq', 'ctx'), 'head'), parts along dimension 0
The draws below stay inside these ranges and needn't reach their ends.
There are 4 independent parts, one for each index of `seq`. The reference program is written for one: setup_inputs(seed, part) draws one part's arguments, and reference() takes and returns one part's arrays. A program takes and returns all parts, laid end to end along the dimension named above; each array names one. Nothing has to cross between parts.
All inputs are finite; a program needn't handle non-finite values.
Results may differ from the reference program's by a relative error of at most 0.0035.
Values may be sent and summed in bfloat16 or wider, within the bound.
No kernel may reach another device: no remote copies, remote signals or barrier semaphores. Data moves between devices by JAX's collectives and lax.ppermute only.
A program may use at most 64 MiB of HBM per device.

```python
import math
import jax
import jax.numpy as jnp
from jax import lax

HD = 128
GROUP = 16
KVH = 4
HQ = 64
SEQ_LEN = 512


def common_pair(key):
    base = jax.random.fold_in(key, 7)
    first, second = jax.random.split(base, 2)
    query_draw = 2.5 * jax.random.truncated_normal(first, -6.0, 6.0, (SEQ_LEN, HQ, HD), jnp.float32)
    key_draw = jax.random.truncated_normal(second, -6.0, 6.0, (SEQ_LEN, KVH, HD), jnp.float32)
    return (query_draw, key_draw)


def draw_queries(key, part):
    return common_pair(key)[0].astype(jnp.bfloat16)


def draw_keys(key, part):
    return common_pair(key)[1].astype(jnp.bfloat16)


def level_of(stream_key, dims, cuts, low, top_value):
    def one(axis_at, shards_of):
        steps = jax.random.uniform(jax.random.fold_in(jax.random.fold_in(stream_key, 6), axis_at), (shards_of,), jnp.float32, low / len(cuts), top_value / len(cuts))
        return jnp.repeat(jnp.exp(steps), dims[axis_at] // shards_of).reshape((-1,) + (1,) * (len(dims) - axis_at - 1))

    level = one(*cuts[0])
    for cut in cuts[1:]:
        level = level * one(*cut)
    return level


def gaussian(key, extent, deviation, most, cuts=(), kind=jnp.bfloat16):
    entries = jax.random.normal(key, extent, jnp.float32) * deviation
    if len(cuts) > 0:
        entries = level_of(key, extent, cuts, -0.22, 0.18) * entries
    return jnp.clip(entries, min=-most, max=most).astype(kind)


def setup_inputs(seed: int = 0, part: int = 0) -> dict:
    streams_of = jax.random.split(jax.random.key(seed), 4)
    own_keys = jax.random.split(jax.random.fold_in(streams_of[3], part), 4)
    queries = draw_queries(jax.random.fold_in(jax.random.fold_in(streams_of[3], part), 71), part)
    keys = draw_keys(jax.random.fold_in(jax.random.fold_in(streams_of[3], part), 71), part)
    values = gaussian(own_keys[2], (SEQ_LEN, KVH, HD), 1.0, 6.0, ((0, 4), (1, 2)))
    return {"queries": queries, "keys": keys, "values": values}


def reference(queries, keys, values):
    seq_total = queries.shape[0]
    block_rows = math.gcd(seq_total, 512)
    scale = 1.0 / math.sqrt(HD)
    key_places = jnp.arange(seq_total, dtype=jnp.int32)
    pieces_out = []
    for head_group in range(KVH):
        key_group = keys[:, head_group, :].astype(jnp.float32)
        value_group = values[:, head_group, :].astype(jnp.float32)
        query_group = queries[:, head_group * GROUP:(head_group + 1) * GROUP, :]
        query_group = query_group.reshape(seq_total // block_rows, block_rows, GROUP, HD)
        firsts = jnp.arange(seq_total // block_rows, dtype=jnp.int32) * block_rows

        def one_block(item):
            query_block, first_row = item
            scores = jnp.einsum('rhd,nd->rhn', query_block.astype(jnp.float32), key_group) * scale
            query_places = first_row + jnp.arange(block_rows, dtype=jnp.int32)
            visible = key_places[None, None, :] <= query_places[:, None, None]
            scores = jnp.where(visible, scores, -1e+30)
            top = lax.optimization_barrier(jnp.max(scores, axis=-1, keepdims=True))
            expo = jnp.where(visible, jnp.exp(scores - top), 0.0)
            total = lax.optimization_barrier(jnp.sum(expo, axis=-1))
            weights = expo.astype(jnp.bfloat16).astype(jnp.float32)
            numer = jnp.einsum('rhn,nd->rhd', weights, value_group)
            return (numer / total[..., None]).astype(jnp.bfloat16)
        result = lax.map(one_block, (query_group, firsts))
        pieces_out.append(result.reshape(seq_total, GROUP, HD))
    return jnp.concatenate(pieces_out, axis=1)
```

```python
import functools
import math

import jax
import jax.numpy as jnp
from jax import lax
from jax.experimental import pallas as pl
from jax.experimental.pallas import tpu as pltpu
from jax.sharding import PartitionSpec as P

VMEM_LIMIT = 30 * 1024 * 1024
TILE_ROWS = 256
NEG = -1e30


def tile_plan(rows, group):
    return math.gcd(rows, max(1, TILE_ROWS // group))


def split_into(packed, kv_heads, base, block_ref):
    total, depth = packed.shape
    count = total // kv_heads
    if kv_heads == 1:
        block_ref[0, base : base + count, :depth] = packed
        return
    rows = lax.broadcasted_iota(jnp.int32, (count, total), 0)
    cols = lax.broadcasted_iota(jnp.int32, (count, total), 1)
    for head in range(kv_heads):
        pick = (cols == rows * kv_heads + head).astype(packed.dtype)
        block = jnp.dot(pick, packed, preferred_element_type=jnp.float32)
        block_ref[head, base : base + count, :depth] = block.astype(packed.dtype)


def fill_ones(values_ref, depth):
    shape = (values_ref.shape[0], values_ref.shape[1], values_ref.shape[2] - depth)
    values_ref[:, :, depth:] = jnp.ones(shape, values_ref.dtype)


def tile_queries(q_ref, head, group, tile, positions):
    rows = q_ref[tile * positions : (tile + 1) * positions, head * group : (head + 1) * group, :]
    return rows.reshape(positions * group, q_ref.shape[2])


def scores_of(q_rows, keys):
    return lax.dot_general(
        q_rows, keys, (((1,), (1,)), ((), ())), preferred_element_type=jnp.float32
    )


def put_result(stage_ref, head, group, tile, positions, numer, total):
    result = (numer * (1.0 / total)).astype(stage_ref.dtype)
    stage_ref[tile * positions : (tile + 1) * positions, head * group : (head + 1) * group, :] = (
        result.reshape(positions, group, numer.shape[1])
    )


def out_copy(stage_ref, out_ref, sems, tile, positions):
    where = pl.ds(tile * positions, positions)
    return pltpu.make_async_copy(stage_ref.at[where], out_ref.at[where], sems.at[tile])


def first_kernel(axis, pair, kv_heads, factor, *refs):
    q_hbm, k_hbm, v_hbm = refs[:3]
    near_refs = refs[3 : 1 + 2 * pair]
    q_ref, top_ref, sums_ref, out_ref = refs[1 + 2 * pair : 5 + 2 * pair]
    own_k, own_v, keys_ref, values_ref, stage_ref, kv_sems, q_sems, out_sems = refs[5 + 2 * pair :]
    rows, heads, depth = q_ref.shape
    group = heads // kv_heads
    positions = tile_plan(rows, group)
    tile_rows = positions * group
    tiles = rows // positions
    me = lax.axis_index(axis)
    lane = lax.rem(me, pair)

    copy_k = pltpu.make_async_copy(k_hbm, own_k, kv_sems.at[0])
    copy_v = pltpu.make_async_copy(v_hbm, own_v, kv_sems.at[1])
    copy_q = pltpu.make_async_copy(q_hbm, q_ref, q_sems.at[0])
    copy_k.start()
    copy_v.start()
    copy_q.start()
    fill_ones(values_ref, depth)
    if pair > 1:
        split_into(near_refs[0][...], kv_heads, rows, keys_ref)
        split_into(near_refs[1][...], kv_heads, rows, values_ref)
    copy_k.wait()
    split_into(own_k[...], kv_heads, 0, keys_ref)
    copy_v.wait()
    split_into(own_v[...], kv_heads, 0, values_ref)
    copy_q.wait()
    bias = jnp.where(lane > 0, 0.0, NEG).astype(jnp.float32)

    for tile in range(tiles):
        for head in range(kv_heads):
            where = slice(tile * tile_rows, (tile + 1) * tile_rows)
            q_rows = tile_queries(q_ref, head, group, tile, positions)
            scores = scores_of(q_rows, keys_ref[head])
            own = scores[:, :rows].reshape(positions, group, rows)
            place = tile * positions + lax.broadcasted_iota(jnp.int32, own.shape, 0)
            own = jnp.where(lax.broadcasted_iota(jnp.int32, own.shape, 2) <= place, own, NEG)
            own = own.reshape(tile_rows, rows)
            if pair > 1:
                scores = jnp.concatenate([own, scores[:, rows:] + bias], axis=1)
            else:
                scores = own
            top = jnp.max(scores, axis=1, keepdims=True)
            weights = jnp.exp2((scores - top) * factor).astype(values_ref.dtype)
            top_ref[head, where, :] = jnp.broadcast_to(top, (tile_rows, depth))
            sums_ref[head, where, :] = jnp.dot(
                weights, values_ref[head], preferred_element_type=jnp.float32
            )

    @pl.when(lax.div(me, pair) == 0)
    def _():
        for tile in range(tiles):
            where = slice(tile * tile_rows, (tile + 1) * tile_rows)
            for head in range(kv_heads):
                put_result(
                    stage_ref, head, group, tile, positions,
                    sums_ref[head, where, :depth], sums_ref[head, where, depth:],
                )
            out_copy(stage_ref, out_ref, out_sems, tile, positions).start()
        for tile in range(tiles):
            out_copy(stage_ref, out_ref, out_sems, tile, positions).wait()


def last_kernel(axis, pair, kv_heads, factor, hop, *refs):
    q_ref = refs[0]
    far_refs = refs[1 : 1 + 2 * pair]
    top_ref, sums_ref = refs[1 + 2 * pair : 3 + 2 * pair]
    out_ref = refs[4 + 2 * pair]
    keys_ref, values_ref, stage_ref, out_sems = refs[5 + 2 * pair :]
    rows, heads, depth = q_ref.shape
    group = heads // kv_heads
    positions = tile_plan(rows, group)
    tile_rows = positions * group
    tiles = rows // positions
    me = lax.axis_index(axis)

    @pl.when(lax.div(me, pair) >= hop)
    def _():
        fill_ones(values_ref, depth)
        for block in range(pair):
            split_into(far_refs[2 * block][...], kv_heads, block * rows, keys_ref)
            split_into(far_refs[2 * block + 1][...], kv_heads, block * rows, values_ref)

        for tile in range(tiles):
            where = slice(tile * tile_rows, (tile + 1) * tile_rows)
            for head in range(kv_heads):
                q_rows = tile_queries(q_ref, head, group, tile, positions)
                scores = scores_of(q_rows, keys_ref[head])
                old = top_ref[head, where, :]
                top = jnp.maximum(jnp.max(scores, axis=1, keepdims=True), old)
                weights = jnp.concatenate(
                    [
                        jnp.exp2((scores[:, at : at + depth] - top) * factor)
                        for at in range(0, scores.shape[1], depth)
                    ],
                    axis=1,
                ).astype(values_ref.dtype)
                rescale = jnp.exp2((old - top) * factor)
                sums = jnp.dot(weights, values_ref[head], preferred_element_type=jnp.float32)
                put_result(
                    stage_ref, head, group, tile, positions,
                    sums_ref[head, where, :depth] * rescale + sums[:, :depth],
                    sums_ref[head, where, depth:] * rescale + sums[:, depth:],
                )
            out_copy(stage_ref, out_ref, out_sems, tile, positions).start()
        for tile in range(tiles):
            out_copy(stage_ref, out_ref, out_sems, tile, positions).wait()


def in_vmem(array):
    return pltpu.with_memory_space_constraint(array, pltpu.VMEM)


def in_hbm(array):
    return pltpu.with_memory_space_constraint(array, pltpu.HBM)


def local(ctx_size, queries, keys, values):
    rows, heads, depth = queries.shape
    kv_heads = keys.shape[1]
    group = heads // kv_heads
    pair = 2 if ctx_size % 2 == 0 else 1
    chips = ctx_size // pair
    factor = math.log2(math.e) / math.sqrt(depth)
    vmem = pl.BlockSpec(memory_space=pltpu.VMEM)
    anywhere = pl.BlockSpec(memory_space=pl.ANY)

    keys = keys.reshape(rows * kv_heads, depth)
    values = values.reshape(rows * kv_heads, depth)
    swap = [(i, i ^ 1) for i in range(ctx_size)]
    hops = [
        [
            (i, (i // pair + hop) % chips * pair + (pair - 1 - i % pair))
            for i in range(ctx_size)
        ]
        for hop in range(chips)
    ]

    far_keys = lax.ppermute(keys, "ctx", hops[1])
    far_values = lax.ppermute(values, "ctx", hops[1])
    near = []
    if pair == 2:
        near = [lax.ppermute(keys, "ctx", swap), lax.ppermute(values, "ctx", swap)]

    positions = tile_plan(rows, group)
    tiles = rows // positions
    work = heads * rows * rows * pair
    cost = pl.CostEstimate(
        flops=work * depth * 4, bytes_accessed=heads * rows * depth * 2, transcendentals=work
    )
    split_scratch = [
        pltpu.VMEM((kv_heads, pair * rows, depth), keys.dtype),
        pltpu.VMEM((kv_heads, pair * rows, 2 * depth), keys.dtype),
        pltpu.VMEM(queries.shape, queries.dtype),
    ]
    q_vmem, top, sums, out = pl.pallas_call(
        functools.partial(first_kernel, "ctx", pair, kv_heads, factor),
        out_shape=(
            pltpu.VMEM(queries.shape, queries.dtype),
            pltpu.VMEM((kv_heads, rows * group, depth), jnp.float32),
            pltpu.VMEM((kv_heads, rows * group, 2 * depth), jnp.float32),
            jax.ShapeDtypeStruct(queries.shape, queries.dtype),
        ),
        in_specs=[anywhere] * 3 + [vmem] * len(near),
        out_specs=(vmem,) * 3 + (anywhere,),
        scratch_shapes=[
            pltpu.VMEM(keys.shape, keys.dtype),
            pltpu.VMEM(keys.shape, keys.dtype),
            *split_scratch,
            pltpu.SemaphoreType.DMA((2,)),
            pltpu.SemaphoreType.DMA((1,)),
            pltpu.SemaphoreType.DMA((tiles,)),
        ],
        compiler_params=pltpu.CompilerParams(vmem_limit_bytes=VMEM_LIMIT),
        cost_estimate=cost,
    )(*[in_hbm(x) for x in (queries, keys, values)], *[in_vmem(x) for x in near])

    far_keys, top = lax.optimization_barrier((far_keys, top))
    far_values, sums = lax.optimization_barrier((far_values, sums))
    far = [far_keys, far_values]
    if pair == 2:
        far += [lax.ppermute(far_keys, "ctx", swap), lax.ppermute(far_values, "ctx", swap)]
    return pl.pallas_call(
        functools.partial(last_kernel, "ctx", pair, kv_heads, factor, 1),
        out_shape=jax.ShapeDtypeStruct(queries.shape, queries.dtype),
        in_specs=[vmem] * (3 + 2 * pair) + [anywhere],
        out_specs=anywhere,
        scratch_shapes=[*split_scratch, pltpu.SemaphoreType.DMA((tiles,))],
        input_output_aliases={3 + 2 * pair: 0},
        compiler_params=pltpu.CompilerParams(vmem_limit_bytes=VMEM_LIMIT),
        cost_estimate=cost,
    )(in_vmem(q_vmem), *[in_vmem(x) for x in far], *[in_vmem(x) for x in (top, sums)], in_hbm(out))


def solution(mesh):
    return jax.shard_map(
        functools.partial(local, mesh.shape["ctx"]),
        mesh=mesh,
        in_specs=(
            P(("seq", "ctx"), "head", None),
            P(("seq", "ctx"), "head", None),
            P(("seq", "ctx"), "head", None),
        ),
        out_specs=P(("seq", "ctx"), "head", None),
        check_vma=False,
    )
```

```python
import functools
import math

import jax
import jax.numpy as jnp
from jax import lax
from jax.experimental import pallas as pl
from jax.experimental.pallas import tpu as pltpu
from jax.sharding import PartitionSpec as P

VMEM_LIMIT = 30 * 1024 * 1024
TILE_ROWS = 256
NEG = -1e30
DIRECT = False


def tile_plan(rows, group):
    return math.gcd(rows, max(1, TILE_ROWS // group))


def split_into(packed, kv_heads, base, wide_ref, block_ref):
    total, depth = packed.shape
    count = total // kv_heads
    if kv_heads == 1:
        block_ref[0, base : base + count, :depth] = packed
        return
    wide_ref[...] = packed.astype(jnp.float32)
    for head in range(kv_heads):
        block = wide_ref[pl.ds(head, count, stride=kv_heads), :]
        block_ref[head, base : base + count, :depth] = block.astype(packed.dtype)


def fill_ones(values_ref, depth):
    shape = (values_ref.shape[0], values_ref.shape[1], values_ref.shape[2] - depth)
    values_ref[:, :, depth:] = jnp.ones(shape, values_ref.dtype)


def tile_queries(q_ref, head, group, tile, positions):
    rows = q_ref[tile * positions : (tile + 1) * positions, head * group : (head + 1) * group, :]
    return rows.reshape(positions * group, q_ref.shape[2])


def scores_of(q_rows, keys):
    return lax.dot_general(
        q_rows, keys, (((1,), (1,)), ((), ())), preferred_element_type=jnp.float32
    )


def put_result(stage_ref, head, group, tile, positions, numer, total):
    result = (numer * (1.0 / total)).astype(stage_ref.dtype)
    stage_ref[tile * positions : (tile + 1) * positions, head * group : (head + 1) * group, :] = (
        result.reshape(positions, group, numer.shape[1])
    )


def out_copy(stage_ref, out_ref, sems, tile, positions):
    where = pl.ds(tile * positions, positions)
    return pltpu.make_async_copy(stage_ref.at[where], out_ref.at[where], sems.at[tile])


def first_kernel(axis, pair, kv_heads, factor, *refs):
    q_hbm, k_hbm, v_hbm = refs[:3]
    near_refs = refs[3 : 1 + 2 * pair]
    q_ref, top_ref, sums_ref = refs[1 + 2 * pair : 4 + 2 * pair]
    own_k, own_v, wide_ref, keys_ref, values_ref, kv_sems, q_sems = refs[4 + 2 * pair :]
    rows, heads, depth = q_ref.shape
    group = heads // kv_heads
    positions = tile_plan(rows, group)
    tile_rows = positions * group
    tiles = rows // positions
    me = lax.axis_index(axis)
    lane = lax.rem(me, pair)

    copy_k = pltpu.make_async_copy(k_hbm, own_k, kv_sems.at[0])
    copy_v = pltpu.make_async_copy(v_hbm, own_v, kv_sems.at[1])
    copy_q = pltpu.make_async_copy(q_hbm, q_ref, q_sems.at[0])
    copy_k.start()
    copy_v.start()
    copy_q.start()
    fill_ones(values_ref, depth)
    if pair > 1:
        split_into(near_refs[0][...], kv_heads, rows, wide_ref.at[0], keys_ref)
        split_into(near_refs[1][...], kv_heads, rows, wide_ref.at[1], values_ref)
    copy_k.wait()
    split_into(own_k[...], kv_heads, 0, wide_ref.at[2], keys_ref)
    copy_v.wait()
    split_into(own_v[...], kv_heads, 0, wide_ref.at[3], values_ref)
    copy_q.wait()
    bias = jnp.where(lane > 0, 0.0, NEG).astype(jnp.float32)

    for tile in range(tiles):
        for head in range(kv_heads):
            where = slice(tile * tile_rows, (tile + 1) * tile_rows)
            q_rows = tile_queries(q_ref, head, group, tile, positions)
            scores = scores_of(q_rows, keys_ref[head])
            own = scores[:, :rows].reshape(positions, group, rows)
            place = tile * positions + lax.broadcasted_iota(jnp.int32, own.shape, 0)
            own = jnp.where(lax.broadcasted_iota(jnp.int32, own.shape, 2) <= place, own, NEG)
            own = own.reshape(tile_rows, rows)
            if pair > 1:
                scores = jnp.concatenate([own, scores[:, rows:] + bias], axis=1)
            else:
                scores = own
            top = jnp.max(scores, axis=1, keepdims=True)
            weights = jnp.exp2((scores - top) * factor).astype(values_ref.dtype)
            top_ref[head, where, :] = jnp.broadcast_to(top, (tile_rows, depth))
            sums_ref[head, where, :] = jnp.dot(
                weights, values_ref[head], preferred_element_type=jnp.float32
            )


def keys_kernel(axis, pair, kv_heads, factor, hop, last, *refs):
    q_ref = refs[0]
    key_refs = refs[1 : 1 + pair]
    old_ref, sums_ref = refs[1 + pair : 3 + pair]
    held = hop > 1
    weights_ref, drop_ref, out_ref = refs[3 + held + pair : 6 + held + pair]
    top_ref = None if last else refs[6 + held + pair]
    wide_ref, keys_ref, stage_ref, out_sems = refs[-4:]
    rows, heads, depth = q_ref.shape
    group = heads // kv_heads
    positions = tile_plan(rows, group)
    tile_rows = positions * group
    tiles = rows // positions
    chip = lax.div(lax.axis_index(axis), pair)

    @pl.when(chip >= hop)
    def _():
        for block in range(pair):
            split_into(key_refs[block][...], kv_heads, block * rows, wide_ref.at[block], keys_ref)
        for tile in range(tiles):
            where = slice(tile * tile_rows, (tile + 1) * tile_rows)
            for head in range(kv_heads):
                q_rows = tile_queries(q_ref, head, group, tile, positions)
                scores = scores_of(q_rows, keys_ref[head])
                old = old_ref[head, where, :]
                top = jnp.maximum(jnp.max(scores, axis=1, keepdims=True), old)
                if top_ref is not None:
                    top_ref[head, where, :] = top
                drop_ref[head, where, :] = (old - top) * factor
                for part in range(pair * rows // depth):
                    weights_ref[head, part, where, :] = jnp.exp2(
                        (scores[:, part * depth : (part + 1) * depth] - top) * factor
                    ).astype(weights_ref.dtype)

    @pl.when(chip == hop - 1)
    def _():
        for tile in range(tiles):
            where = slice(tile * tile_rows, (tile + 1) * tile_rows)
            for head in range(kv_heads):
                put_result(
                    stage_ref, head, group, tile, positions,
                    sums_ref[head, where, :depth], sums_ref[head, where, depth:],
                )
            out_copy(stage_ref, out_ref, out_sems, tile, positions).start()
        for tile in range(tiles):
            out_copy(stage_ref, out_ref, out_sems, tile, positions).wait()


def values_kernel(axis, pair, kv_heads, hop, last, *refs):
    value_refs = refs[:pair]
    weights_ref, drop_ref, old_ref = refs[pair : 3 + pair]
    sums_ref, out_ref = refs[4 + pair : 6 + pair]
    wide_ref, values_ref, stage_ref, out_sems = refs[6 + pair :]
    rows, heads, depth = stage_ref.shape
    group = heads // kv_heads
    positions = tile_plan(rows, group)
    tile_rows = positions * group
    tiles = rows // positions
    chip = lax.div(lax.axis_index(axis), pair)

    def merged(head, tile):
        where = slice(tile * tile_rows, (tile + 1) * tile_rows)
        weights = jnp.concatenate(
            [weights_ref[head, part, where, :] for part in range(pair * rows // depth)], axis=1
        )
        sums = jnp.dot(weights, values_ref[head], preferred_element_type=jnp.float32)
        rescale = jnp.exp2(drop_ref[head, where, :])
        return (
            old_ref[head, where, :depth] * rescale + sums[:, :depth],
            old_ref[head, where, depth:] * rescale + sums[:, depth:],
        )

    @pl.when(chip >= hop)
    def _():
        fill_ones(values_ref, depth)
        for block in range(pair):
            split_into(value_refs[block][...], kv_heads, block * rows, wide_ref.at[block], values_ref)
        for tile in range(tiles):
            where = slice(tile * tile_rows, (tile + 1) * tile_rows)
            for head in range(kv_heads):
                numer, total = merged(head, tile)
                if last:
                    put_result(stage_ref, head, group, tile, positions, numer, total)
                else:
                    sums_ref[head, where, :depth] = numer
                    sums_ref[head, where, depth:] = total
            if last:
                out_copy(stage_ref, out_ref, out_sems, tile, positions).start()
        if last:
            for tile in range(tiles):
                out_copy(stage_ref, out_ref, out_sems, tile, positions).wait()


def in_vmem(array):
    return pltpu.with_memory_space_constraint(array, pltpu.VMEM)


def in_hbm(array):
    return pltpu.with_memory_space_constraint(array, pltpu.HBM)


def local(ctx_size, queries, keys, values):
    rows, heads, depth = queries.shape
    kv_heads = keys.shape[1]
    group = heads // kv_heads
    pair = 2 if ctx_size % 2 == 0 else 1
    chips = ctx_size // pair
    factor = math.log2(math.e) / math.sqrt(depth)
    vmem = pl.BlockSpec(memory_space=pltpu.VMEM)
    anywhere = pl.BlockSpec(memory_space=pl.ANY)

    keys = keys.reshape(rows * kv_heads, depth)
    values = values.reshape(rows * kv_heads, depth)
    swap = [(i, i ^ 1) for i in range(ctx_size)]

    def across(array, hop, cross):
        route = [
            (i, (i // pair + hop) % chips * pair + (i % pair ^ cross)) for i in range(ctx_size)
        ]
        return lax.ppermute(array, "ctx", route)

    def far_pair(hop):
        far_keys = [across(keys, hop, pair - 1)]
        far_values = [across(values, hop, pair - 1)]
        if pair == 2 and DIRECT:
            far_values.append(across(values, hop, 0))
        return far_keys, far_values

    far = [far_pair(1)]
    near = []
    if pair == 2:
        near = [lax.ppermute(keys, "ctx", swap), lax.ppermute(values, "ctx", swap)]

    positions = tile_plan(rows, group)
    tiles = rows // positions
    work = heads * rows * rows * pair
    cost = pl.CostEstimate(
        flops=work * depth * 4, bytes_accessed=heads * rows * depth * 2, transcendentals=work
    )
    def wide_scratch(count):
        return pltpu.VMEM((count, *keys.shape), jnp.float32)

    keys_scratch = pltpu.VMEM((kv_heads, pair * rows, depth), keys.dtype)
    values_scratch = pltpu.VMEM((kv_heads, pair * rows, 2 * depth), keys.dtype)
    out_scratch = [pltpu.VMEM(queries.shape, queries.dtype), pltpu.SemaphoreType.DMA((tiles,))]
    params = pltpu.CompilerParams(vmem_limit_bytes=VMEM_LIMIT)
    out_shape = jax.ShapeDtypeStruct(queries.shape, queries.dtype)
    top_shape = pltpu.VMEM((kv_heads, rows * group, depth), jnp.float32)
    sums_shape = pltpu.VMEM((kv_heads, rows * group, 2 * depth), jnp.float32)
    weights_shape = pltpu.VMEM(
        (kv_heads, pair * rows // depth, rows * group, depth), values.dtype
    )
    q_vmem, top, sums = pl.pallas_call(
        functools.partial(first_kernel, "ctx", pair, kv_heads, factor),
        out_shape=(pltpu.VMEM(queries.shape, queries.dtype), top_shape, sums_shape),
        in_specs=[anywhere] * 3 + [vmem] * len(near),
        out_specs=(vmem,) * 3,
        scratch_shapes=[
            pltpu.VMEM(keys.shape, keys.dtype),
            pltpu.VMEM(keys.shape, keys.dtype),
            wide_scratch(2 * pair),
            keys_scratch,
            values_scratch,
            pltpu.SemaphoreType.DMA((2,)),
            pltpu.SemaphoreType.DMA((1,)),
        ],
        compiler_params=params,
        cost_estimate=cost,
    )(*[in_hbm(x) for x in (queries, keys, values)], *[in_vmem(x) for x in near])

    out = None
    for hop in range(1, chips):
        last = hop == chips - 1
        if not last:
            far.append(far_pair(hop + 1))
        all_keys, all_values = far[hop - 1]
        first_keys, top = lax.optimization_barrier((all_keys[0], top))
        all_keys = [first_keys]
        if pair == 2:
            all_keys.append(lax.ppermute(first_keys, "ctx", swap))
            if not DIRECT:
                all_keys[1], first_values = lax.optimization_barrier((all_keys[1], all_values[0]))
                all_values = [first_values, lax.ppermute(first_values, "ctx", swap)]
        held = [] if out is None else [in_hbm(out)]
        weights, drop, out, *new_top = pl.pallas_call(
            functools.partial(keys_kernel, "ctx", pair, kv_heads, factor, hop, last),
            out_shape=(weights_shape, top_shape, out_shape) + (() if last else (top_shape,)),
            in_specs=[vmem] * (3 + pair) + [anywhere] * len(held),
            out_specs=(vmem, vmem, anywhere) + (() if last else (vmem,)),
            scratch_shapes=[wide_scratch(pair), keys_scratch, *out_scratch],
            input_output_aliases={3 + pair: 2} if held else {},
            compiler_params=params,
            cost_estimate=cost,
        )(
            in_vmem(q_vmem),
            *[in_vmem(x) for x in all_keys],
            in_vmem(top),
            in_vmem(sums),
            *held,
        )
        top = top if last else new_top[0]
        sums, out = pl.pallas_call(
            functools.partial(values_kernel, "ctx", pair, kv_heads, hop, last),
            out_shape=(sums_shape, out_shape),
            in_specs=[vmem] * (3 + pair) + [anywhere],
            out_specs=(vmem, anywhere),
            scratch_shapes=[wide_scratch(pair), values_scratch, *out_scratch],
            input_output_aliases={2 + pair: 0, 3 + pair: 1},
            compiler_params=params,
            cost_estimate=cost,
        )(
            *[in_vmem(x) for x in all_values],
            *[in_vmem(x) for x in (weights, drop, sums)],
            in_hbm(out),
        )
    return out


def solution(mesh):
    return jax.shard_map(
        functools.partial(local, mesh.shape["ctx"]),
        mesh=mesh,
        in_specs=(
            P(("seq", "ctx"), "head", None),
            P(("seq", "ctx"), "head", None),
            P(("seq", "ctx"), "head", None),
        ),
        out_specs=P(("seq", "ctx"), "head", None),
        check_vma=False,
    )
```

```python
import functools
import math

import jax
import jax.numpy as jnp
from jax import lax
from jax.experimental import pallas as pl
from jax.experimental.pallas import tpu as pltpu
from jax.sharding import PartitionSpec as P

VMEM_LIMIT = 30 * 1024 * 1024
TILE_ROWS = 512
NEG = -1e30
DIRECT = False


def tile_plan(rows, group):
    return math.gcd(rows, max(1, TILE_ROWS // group))


def split_into(packed, kv_heads, base, wide_ref, block_ref):
    total, depth = packed.shape
    count = total // kv_heads
    if kv_heads == 1:
        block_ref[0, base : base + count, :depth] = packed
        return
    wide_ref[...] = packed.astype(jnp.float32)
    for head in range(kv_heads):
        block = wide_ref[pl.ds(head, count, stride=kv_heads), :]
        block_ref[head, base : base + count, :depth] = block.astype(packed.dtype)


def fill_ones(values_ref, depth):
    shape = (values_ref.shape[0], values_ref.shape[1], values_ref.shape[2] - depth)
    values_ref[:, :, depth:] = jnp.ones(shape, values_ref.dtype)


def tile_queries(q_ref, head, group, tile, positions):
    rows = q_ref[tile * positions : (tile + 1) * positions, head * group : (head + 1) * group, :]
    return rows.reshape(positions * group, q_ref.shape[2])


def scores_of(q_rows, keys):
    return lax.dot_general(
        q_rows, keys, (((1,), (1,)), ((), ())), preferred_element_type=jnp.float32
    )


def put_result(stage_ref, head, group, tile, positions, numer, total):
    result = (numer * (1.0 / total)).astype(stage_ref.dtype)
    stage_ref[tile * positions : (tile + 1) * positions, head * group : (head + 1) * group, :] = (
        result.reshape(positions, group, numer.shape[1])
    )


def out_copy(stage_ref, out_ref, sems, tile, positions):
    where = pl.ds(tile * positions, positions)
    return pltpu.make_async_copy(stage_ref.at[where], out_ref.at[where], sems.at[tile])


def load_kernel(kv_heads, *refs):
    k_hbm, v_hbm, keys_ref, values_ref, own_k, own_v, wide_ref, sems = refs
    copies = [
        pltpu.make_async_copy(source, target, sems.at[i])
        for i, (source, target) in enumerate(((k_hbm, own_k), (v_hbm, own_v)))
    ]
    for copy in copies:
        copy.start()
    fill_ones(values_ref, keys_ref.shape[2])
    copies[0].wait()
    split_into(own_k[...], kv_heads, 0, wide_ref.at[0], keys_ref)
    copies[1].wait()
    split_into(own_v[...], kv_heads, 0, wide_ref.at[1], values_ref)


def first_kernel(axis, pair, kv_heads, factor, *refs):
    q_ref, own_keys_ref, own_values_ref = refs[:3]
    near_refs = refs[3 : 1 + 2 * pair]
    top_ref, sums_ref = refs[1 + 2 * pair : 3 + 2 * pair]
    wide_ref, keys_ref, values_ref = refs[3 + 2 * pair :]
    rows, heads, depth = q_ref.shape
    group = heads // kv_heads
    positions = tile_plan(rows, group)
    tile_rows = positions * group
    tiles = rows // positions
    lane = lax.rem(lax.axis_index(axis), pair)

    keys_ref[:, :rows, :] = own_keys_ref[...]
    values_ref[:, :rows, :] = own_values_ref[...]
    if pair > 1:
        fill_ones(values_ref.at[:, rows:], depth)
        split_into(near_refs[0][...], kv_heads, rows, wide_ref.at[0], keys_ref)
        split_into(near_refs[1][...], kv_heads, rows, wide_ref.at[1], values_ref)
    bias = jnp.where(lane > 0, 0.0, NEG).astype(jnp.float32)

    for tile in range(tiles):
        for head in range(kv_heads):
            where = slice(tile * tile_rows, (tile + 1) * tile_rows)
            q_rows = tile_queries(q_ref, head, group, tile, positions)
            scores = scores_of(q_rows, keys_ref[head])
            own = scores[:, :rows].reshape(positions, group, rows)
            place = tile * positions + lax.broadcasted_iota(jnp.int32, own.shape, 0)
            own = jnp.where(lax.broadcasted_iota(jnp.int32, own.shape, 2) <= place, own, NEG)
            own = own.reshape(tile_rows, rows)
            if pair > 1:
                scores = jnp.concatenate([own, scores[:, rows:] + bias], axis=1)
            else:
                scores = own
            top = jnp.max(scores, axis=1, keepdims=True)
            weights = jnp.exp2((scores - top) * factor).astype(values_ref.dtype)
            top_ref[head, where, :] = jnp.broadcast_to(top, (tile_rows, depth))
            sums_ref[head, where, :] = jnp.dot(
                weights, values_ref[head], preferred_element_type=jnp.float32
            )


def keys_kernel(axis, pair, kv_heads, factor, hop, last, *refs):
    q_ref = refs[0]
    key_refs = refs[1 : 1 + pair]
    old_ref, sums_ref = refs[1 + pair : 3 + pair]
    held = hop > 1
    weights_ref, drop_ref, out_ref = refs[3 + held + pair : 6 + held + pair]
    top_ref = None if last else refs[6 + held + pair]
    wide_ref, keys_ref, stage_ref, out_sems = refs[-4:]
    rows, heads, depth = q_ref.shape
    group = heads // kv_heads
    positions = tile_plan(rows, group)
    tile_rows = positions * group
    tiles = rows // positions
    chip = lax.div(lax.axis_index(axis), pair)

    @pl.when(chip >= hop)
    def _():
        for block in range(pair):
            split_into(key_refs[block][...], kv_heads, block * rows, wide_ref.at[block], keys_ref)
        for tile in range(tiles):
            where = slice(tile * tile_rows, (tile + 1) * tile_rows)
            for head in range(kv_heads):
                q_rows = tile_queries(q_ref, head, group, tile, positions)
                scores = scores_of(q_rows, keys_ref[head])
                old = old_ref[head, where, :]
                top = jnp.maximum(jnp.max(scores, axis=1, keepdims=True), old)
                if top_ref is not None:
                    top_ref[head, where, :] = top
                drop_ref[head, where, :] = (old - top) * factor
                for part in range(pair * rows // depth):
                    weights_ref[head, part, where, :] = jnp.exp2(
                        (scores[:, part * depth : (part + 1) * depth] - top) * factor
                    ).astype(weights_ref.dtype)

    @pl.when(chip == hop - 1)
    def _():
        for tile in range(tiles):
            where = slice(tile * tile_rows, (tile + 1) * tile_rows)
            for head in range(kv_heads):
                put_result(
                    stage_ref, head, group, tile, positions,
                    sums_ref[head, where, :depth], sums_ref[head, where, depth:],
                )
            out_copy(stage_ref, out_ref, out_sems, tile, positions).start()
        for tile in range(tiles):
            out_copy(stage_ref, out_ref, out_sems, tile, positions).wait()


def values_kernel(axis, pair, kv_heads, hop, last, *refs):
    value_refs = refs[:pair]
    weights_ref, drop_ref, old_ref = refs[pair : 3 + pair]
    sums_ref, out_ref = refs[4 + pair : 6 + pair]
    wide_ref, values_ref, stage_ref, out_sems = refs[6 + pair :]
    rows, heads, depth = stage_ref.shape
    group = heads // kv_heads
    positions = tile_plan(rows, group)
    tile_rows = positions * group
    tiles = rows // positions
    chip = lax.div(lax.axis_index(axis), pair)

    def merged(head, tile):
        where = slice(tile * tile_rows, (tile + 1) * tile_rows)
        weights = jnp.concatenate(
            [weights_ref[head, part, where, :] for part in range(pair * rows // depth)], axis=1
        )
        sums = jnp.dot(weights, values_ref[head], preferred_element_type=jnp.float32)
        rescale = jnp.exp2(drop_ref[head, where, :])
        return (
            old_ref[head, where, :depth] * rescale + sums[:, :depth],
            old_ref[head, where, depth:] * rescale + sums[:, depth:],
        )

    @pl.when(chip >= hop)
    def _():
        fill_ones(values_ref, depth)
        for block in range(pair):
            split_into(value_refs[block][...], kv_heads, block * rows, wide_ref.at[block], values_ref)
        for tile in range(tiles):
            where = slice(tile * tile_rows, (tile + 1) * tile_rows)
            for head in range(kv_heads):
                numer, total = merged(head, tile)
                if last:
                    put_result(stage_ref, head, group, tile, positions, numer, total)
                else:
                    sums_ref[head, where, :depth] = numer
                    sums_ref[head, where, depth:] = total
            if last:
                out_copy(stage_ref, out_ref, out_sems, tile, positions).start()
        if last:
            for tile in range(tiles):
                out_copy(stage_ref, out_ref, out_sems, tile, positions).wait()


def in_vmem(array):
    return pltpu.with_memory_space_constraint(array, pltpu.VMEM)


def in_hbm(array):
    return pltpu.with_memory_space_constraint(array, pltpu.HBM)


def local(ctx_size, queries, keys, values):
    rows, heads, depth = queries.shape
    kv_heads = keys.shape[1]
    group = heads // kv_heads
    pair = 2 if ctx_size % 2 == 0 else 1
    chips = ctx_size // pair
    factor = math.log2(math.e) / math.sqrt(depth)
    vmem = pl.BlockSpec(memory_space=pltpu.VMEM)
    anywhere = pl.BlockSpec(memory_space=pl.ANY)

    raw_keys, raw_values = keys, values
    keys = keys.reshape(rows * kv_heads, depth)
    values = values.reshape(rows * kv_heads, depth)
    swap = [(i, i ^ 1) for i in range(ctx_size)]

    def across(array, hop, cross):
        route = [
            (i, (i // pair + hop) % chips * pair + (i % pair ^ cross)) for i in range(ctx_size)
        ]
        return lax.ppermute(array, "ctx", route).reshape(rows * kv_heads, depth)

    def far_pair(hop):
        far_keys = [across(raw_keys, hop, pair - 1)]
        far_values = [across(values, hop, pair - 1)]
        if pair == 2 and DIRECT:
            far_values.append(across(values, hop, 0))
        return far_keys, far_values

    far = [far_pair(1)]
    near = []
    if pair == 2:
        near_values = lax.ppermute(raw_values, "ctx", swap).reshape(rows * kv_heads, depth)
        near = [lax.ppermute(keys, "ctx", swap), near_values]

    positions = tile_plan(rows, group)
    tiles = rows // positions
    work = heads * rows * rows * pair
    cost = pl.CostEstimate(
        flops=work * depth * 4, bytes_accessed=heads * rows * depth * 2, transcendentals=work
    )
    def wide_scratch(count):
        return pltpu.VMEM((count, *keys.shape), jnp.float32)

    keys_scratch = pltpu.VMEM((kv_heads, pair * rows, depth), keys.dtype)
    values_scratch = pltpu.VMEM((kv_heads, pair * rows, 2 * depth), keys.dtype)
    out_scratch = [pltpu.VMEM(queries.shape, queries.dtype), pltpu.SemaphoreType.DMA((tiles,))]
    params = pltpu.CompilerParams(vmem_limit_bytes=VMEM_LIMIT)
    out_shape = jax.ShapeDtypeStruct(queries.shape, queries.dtype)
    top_shape = pltpu.VMEM((kv_heads, rows * group, depth), jnp.float32)
    sums_shape = pltpu.VMEM((kv_heads, rows * group, 2 * depth), jnp.float32)
    weights_shape = pltpu.VMEM(
        (kv_heads, pair * rows // depth, rows * group, depth), values.dtype
    )
    q_vmem = queries
    own_keys, own_values = pl.pallas_call(
        functools.partial(load_kernel, kv_heads),
        out_shape=(
            pltpu.VMEM((kv_heads, rows, depth), keys.dtype),
            pltpu.VMEM((kv_heads, rows, 2 * depth), values.dtype),
        ),
        in_specs=[anywhere] * 2,
        out_specs=(vmem,) * 2,
        scratch_shapes=[
            pltpu.VMEM(keys.shape, keys.dtype),
            pltpu.VMEM(values.shape, values.dtype),
            wide_scratch(2),
            pltpu.SemaphoreType.DMA((2,)),
        ],
        compiler_params=params,
        cost_estimate=pl.CostEstimate(flops=work * depth * 400, bytes_accessed=heads * rows * depth * 200, transcendentals=work),
    )(*[in_hbm(x) for x in (keys, values)])
    top, sums = pl.pallas_call(
        functools.partial(first_kernel, "ctx", pair, kv_heads, factor),
        out_shape=(top_shape, sums_shape),
        in_specs=[vmem] * (3 + len(near)),
        out_specs=(vmem,) * 2,
        scratch_shapes=[wide_scratch(2), keys_scratch, values_scratch],
        compiler_params=params,
        cost_estimate=pl.CostEstimate(flops=work * depth * 400, bytes_accessed=heads * rows * depth * 200, transcendentals=work),
    )(*[in_vmem(x) for x in (q_vmem, own_keys, own_values, *near)])

    out = None
    for hop in range(1, chips):
        last = hop == chips - 1
        if not last:
            far.append(far_pair(hop + 1))
        all_keys, all_values = far[hop - 1]
        first_keys, top = lax.optimization_barrier((all_keys[0], top))
        all_keys = [first_keys]
        if pair == 2:
            all_keys.append(lax.ppermute(first_keys, "ctx", swap))
            if not DIRECT:
                all_keys[1], first_values = lax.optimization_barrier((all_keys[1], all_values[0]))
                all_values = [first_values, lax.ppermute(first_values, "ctx", swap)]
        held = [] if out is None else [in_hbm(out)]
        weights, drop, out, *new_top = pl.pallas_call(
            functools.partial(keys_kernel, "ctx", pair, kv_heads, factor, hop, last),
            out_shape=(weights_shape, top_shape, out_shape) + (() if last else (top_shape,)),
            in_specs=[vmem] * (3 + pair) + [anywhere] * len(held),
            out_specs=(vmem, vmem, anywhere) + (() if last else (vmem,)),
            scratch_shapes=[wide_scratch(pair), keys_scratch, *out_scratch],
            input_output_aliases={3 + pair: 2} if held else {},
            compiler_params=params,
            cost_estimate=cost,
        )(
            in_vmem(q_vmem),
            *[in_vmem(x) for x in all_keys],
            in_vmem(top),
            in_vmem(sums),
            *held,
        )
        top = top if last else new_top[0]
        sums, out = pl.pallas_call(
            functools.partial(values_kernel, "ctx", pair, kv_heads, hop, last),
            out_shape=(sums_shape, out_shape),
            in_specs=[vmem] * (3 + pair) + [anywhere],
            out_specs=(vmem, anywhere),
            scratch_shapes=[wide_scratch(pair), values_scratch, *out_scratch],
            input_output_aliases={2 + pair: 0, 3 + pair: 1},
            compiler_params=params,
            cost_estimate=cost,
        )(
            *[in_vmem(x) for x in all_values],
            *[in_vmem(x) for x in (weights, drop, sums)],
            in_hbm(out),
        )
    return out


def solution(mesh):
    return jax.shard_map(
        functools.partial(local, mesh.shape["ctx"]),
        mesh=mesh,
        in_specs=(
            P(("seq", "ctx"), "head", None),
            P(("seq", "ctx"), "head", None),
            P(("seq", "ctx"), "head", None),
        ),
        out_specs=P(("seq", "ctx"), "head", None),
        check_vma=False,
    )
```

```python
import functools
import math

import jax
import jax.numpy as jnp
from jax import lax
from jax.experimental import pallas as pl
from jax.experimental.pallas import tpu as pltpu
from jax.sharding import PartitionSpec as P

VMEM_LIMIT = 30 * 1024 * 1024
TILE_ROWS = 512
NEG = -1e30
DIRECT = False


def tile_plan(rows, group):
    return math.gcd(rows, max(1, TILE_ROWS // group))


def split_into(packed, kv_heads, base, wide_ref, block_ref):
    total, depth = packed.shape
    count = total // kv_heads
    if kv_heads == 1:
        block_ref[0, base : base + count, :depth] = packed
        return
    wide_ref[...] = packed.astype(jnp.float32)
    for head in range(kv_heads):
        block = wide_ref[pl.ds(head, count, stride=kv_heads), :]
        block_ref[head, base : base + count, :depth] = block.astype(packed.dtype)


def split_keys(packed, kv_heads, factor, base, wide_ref, keys_ref):
    total, depth = packed.shape
    count = total // kv_heads
    wide_ref[...] = packed.astype(jnp.float32) * factor
    for head in range(kv_heads):
        block = wide_ref[pl.ds(head, count, stride=kv_heads), :]
        high = block.astype(packed.dtype)
        keys_ref[head, base : base + count, :depth] = high
        keys_ref[head, base : base + count, depth:] = (
            block - high.astype(jnp.float32)
        ).astype(packed.dtype)


def fill_ones(values_ref, depth):
    shape = (values_ref.shape[0], values_ref.shape[1], values_ref.shape[2] - depth)
    values_ref[:, :, depth:] = jnp.ones(shape, values_ref.dtype)


def tile_queries(q_ref, head, group, tile, positions):
    rows = q_ref[tile * positions : (tile + 1) * positions, head * group : (head + 1) * group, :]
    return rows.reshape(positions * group, q_ref.shape[2])


def scores_of(q_rows, keys):
    return lax.dot_general(
        q_rows, keys, (((1,), (1,)), ((), ())), preferred_element_type=jnp.float32
    )


def put_result(stage_ref, head, group, tile, positions, numer, total):
    result = (numer * (1.0 / total)).astype(stage_ref.dtype)
    stage_ref[tile * positions : (tile + 1) * positions, head * group : (head + 1) * group, :] = (
        result.reshape(positions, group, numer.shape[1])
    )


def out_copy(stage_ref, out_ref, sems, tile, positions):
    where = pl.ds(tile * positions, positions)
    return pltpu.make_async_copy(stage_ref.at[where], out_ref.at[where], sems.at[tile])


def load_kernel(kv_heads, *refs):
    k_hbm, v_hbm, keys_ref, values_ref, own_k, own_v, wide_ref, sems = refs
    copies = [
        pltpu.make_async_copy(source, target, sems.at[i])
        for i, (source, target) in enumerate(((k_hbm, own_k), (v_hbm, own_v)))
    ]
    for copy in copies:
        copy.start()
    fill_ones(values_ref, keys_ref.shape[2])
    copies[0].wait()
    split_into(own_k[...], kv_heads, 0, wide_ref.at[0], keys_ref)
    copies[1].wait()
    split_into(own_v[...], kv_heads, 0, wide_ref.at[1], values_ref)


def first_kernel(axis, pair, kv_heads, factor, *refs):
    q_ref, own_keys_ref, own_values_ref = refs[:3]
    near_refs = refs[3 : 1 + 2 * pair]
    top_ref, sums_ref = refs[1 + 2 * pair : 3 + 2 * pair]
    wide_ref, keys_ref, values_ref = refs[3 + 2 * pair :]
    rows, heads, depth = q_ref.shape
    group = heads // kv_heads
    positions = tile_plan(rows, group)
    tile_rows = positions * group
    tiles = rows // positions
    lane = lax.rem(lax.axis_index(axis), pair)

    keys_ref[:, :rows, :] = own_keys_ref[...]
    values_ref[:, :rows, :] = own_values_ref[...]
    if pair > 1:
        fill_ones(values_ref.at[:, rows:], depth)
        split_into(near_refs[0][...], kv_heads, rows, wide_ref.at[0], keys_ref)
        split_into(near_refs[1][...], kv_heads, rows, wide_ref.at[1], values_ref)
    bias = jnp.where(lane > 0, 0.0, NEG).astype(jnp.float32)

    for tile in range(tiles):
        for head in range(kv_heads):
            where = slice(tile * tile_rows, (tile + 1) * tile_rows)
            q_rows = tile_queries(q_ref, head, group, tile, positions)
            scores = scores_of(q_rows, keys_ref[head])
            own = scores[:, :rows].reshape(positions, group, rows)
            place = tile * positions + lax.broadcasted_iota(jnp.int32, own.shape, 0)
            own = jnp.where(lax.broadcasted_iota(jnp.int32, own.shape, 2) <= place, own, NEG)
            own = own.reshape(tile_rows, rows)
            if pair > 1:
                scores = jnp.concatenate([own, scores[:, rows:] + bias], axis=1)
            else:
                scores = own
            top = jnp.max(scores, axis=1, keepdims=True)
            weights = jnp.exp2((scores - top) * factor).astype(values_ref.dtype)
            top_ref[head, where, :] = jnp.broadcast_to(top * factor, (tile_rows, depth))
            sums_ref[head, where, :] = jnp.dot(
                weights, values_ref[head], preferred_element_type=jnp.float32
            )


def keys_kernel(axis, pair, kv_heads, factor, hop, last, *refs):
    q_ref = refs[0]
    key_refs = refs[1 : 1 + pair]
    old_ref, sums_ref = refs[1 + pair : 3 + pair]
    held = hop > 1
    weights_ref, drop_ref, out_ref = refs[3 + held + pair : 6 + held + pair]
    top_ref = None if last else refs[6 + held + pair]
    wide_ref, keys_ref, stage_ref, out_sems = refs[-4:]
    rows, heads, depth = q_ref.shape
    group = heads // kv_heads
    positions = tile_plan(rows, group)
    tile_rows = positions * group
    tiles = rows // positions
    chip = lax.div(lax.axis_index(axis), pair)

    @pl.when(chip >= hop)
    def _():
        for block in range(pair):
            split_keys(
                key_refs[block][...], kv_heads, factor, block * rows, wide_ref.at[block], keys_ref
            )
        for tile in range(tiles):
            where = slice(tile * tile_rows, (tile + 1) * tile_rows)
            for head in range(kv_heads):
                q_rows = tile_queries(q_ref, head, group, tile, positions)
                scores = scores_of(jnp.concatenate([q_rows, q_rows], axis=1), keys_ref[head])
                old = old_ref[head, where, :]
                top = jnp.maximum(jnp.max(scores, axis=1, keepdims=True), old)
                if top_ref is not None:
                    top_ref[head, where, :] = top
                drop_ref[head, where, :] = old - top
                for part in range(pair * rows // depth):
                    weights_ref[head, part, where, :] = jnp.exp2(
                        scores[:, part * depth : (part + 1) * depth] - top
                    ).astype(weights_ref.dtype)

    @pl.when(chip == hop - 1)
    def _():
        for tile in range(tiles):
            where = slice(tile * tile_rows, (tile + 1) * tile_rows)
            for head in range(kv_heads):
                put_result(
                    stage_ref, head, group, tile, positions,
                    sums_ref[head, where, :depth], sums_ref[head, where, depth:],
                )
            out_copy(stage_ref, out_ref, out_sems, tile, positions).start()
        for tile in range(tiles):
            out_copy(stage_ref, out_ref, out_sems, tile, positions).wait()


def values_kernel(axis, pair, kv_heads, hop, last, *refs):
    value_refs = refs[:pair]
    weights_ref, drop_ref, old_ref = refs[pair : 3 + pair]
    sums_ref, out_ref = refs[4 + pair : 6 + pair]
    wide_ref, values_ref, stage_ref, out_sems = refs[6 + pair :]
    rows, heads, depth = stage_ref.shape
    group = heads // kv_heads
    positions = tile_plan(rows, group)
    tile_rows = positions * group
    tiles = rows // positions
    chip = lax.div(lax.axis_index(axis), pair)

    def merged(head, tile):
        where = slice(tile * tile_rows, (tile + 1) * tile_rows)
        weights = jnp.concatenate(
            [weights_ref[head, part, where, :] for part in range(pair * rows // depth)], axis=1
        )
        sums = jnp.dot(weights, values_ref[head], preferred_element_type=jnp.float32)
        rescale = jnp.exp2(drop_ref[head, where, :])
        return (
            old_ref[head, where, :depth] * rescale + sums[:, :depth],
            old_ref[head, where, depth:] * rescale + sums[:, depth:],
        )

    @pl.when(chip >= hop)
    def _():
        fill_ones(values_ref, depth)
        for block in range(pair):
            split_into(value_refs[block][...], kv_heads, block * rows, wide_ref.at[block], values_ref)
        for tile in range(tiles):
            where = slice(tile * tile_rows, (tile + 1) * tile_rows)
            for head in range(kv_heads):
                numer, total = merged(head, tile)
                if last:
                    put_result(stage_ref, head, group, tile, positions, numer, total)
                else:
                    sums_ref[head, where, :depth] = numer
                    sums_ref[head, where, depth:] = total
            if last:
                out_copy(stage_ref, out_ref, out_sems, tile, positions).start()
        if last:
            for tile in range(tiles):
                out_copy(stage_ref, out_ref, out_sems, tile, positions).wait()


def in_vmem(array):
    return pltpu.with_memory_space_constraint(array, pltpu.VMEM)


def in_hbm(array):
    return pltpu.with_memory_space_constraint(array, pltpu.HBM)


def local(ctx_size, queries, keys, values):
    rows, heads, depth = queries.shape
    kv_heads = keys.shape[1]
    group = heads // kv_heads
    pair = 2 if ctx_size % 2 == 0 else 1
    chips = ctx_size // pair
    factor = math.log2(math.e) / math.sqrt(depth)
    vmem = pl.BlockSpec(memory_space=pltpu.VMEM)
    anywhere = pl.BlockSpec(memory_space=pl.ANY)

    raw_keys, raw_values = keys, values
    keys = keys.reshape(rows * kv_heads, depth)
    values = values.reshape(rows * kv_heads, depth)
    swap = [(i, i ^ 1) for i in range(ctx_size)]

    def across(array, hop, cross):
        route = [
            (i, (i // pair + hop) % chips * pair + (i % pair ^ cross)) for i in range(ctx_size)
        ]
        return lax.ppermute(array, "ctx", route).reshape(rows * kv_heads, depth)

    def far_pair(hop):
        far_keys = [across(raw_keys, hop, pair - 1)]
        far_values = [across(values, hop, pair - 1)]
        if pair == 2 and DIRECT:
            far_values.append(across(values, hop, 0))
        return far_keys, far_values

    far = [far_pair(1)]
    near = []
    if pair == 2:
        near_values = lax.ppermute(raw_values, "ctx", swap).reshape(rows * kv_heads, depth)
        near = [lax.ppermute(keys, "ctx", swap), near_values]

    positions = tile_plan(rows, group)
    tiles = rows // positions
    work = heads * rows * rows * pair
    cost = pl.CostEstimate(
        flops=work * depth * 4, bytes_accessed=heads * rows * depth * 2, transcendentals=work
    )
    def wide_scratch(count):
        return pltpu.VMEM((count, *keys.shape), jnp.float32)

    keys_scratch = pltpu.VMEM((kv_heads, pair * rows, depth), keys.dtype)
    parts_scratch = pltpu.VMEM((kv_heads, pair * rows, 2 * depth), keys.dtype)
    values_scratch = pltpu.VMEM((kv_heads, pair * rows, 2 * depth), keys.dtype)
    out_scratch = [pltpu.VMEM(queries.shape, queries.dtype), pltpu.SemaphoreType.DMA((tiles,))]
    params = pltpu.CompilerParams(vmem_limit_bytes=VMEM_LIMIT)
    out_shape = jax.ShapeDtypeStruct(queries.shape, queries.dtype)
    top_shape = pltpu.VMEM((kv_heads, rows * group, depth), jnp.float32)
    sums_shape = pltpu.VMEM((kv_heads, rows * group, 2 * depth), jnp.float32)
    weights_shape = pltpu.VMEM(
        (kv_heads, pair * rows // depth, rows * group, depth), values.dtype
    )
    q_vmem = queries
    own_keys, own_values = pl.pallas_call(
        functools.partial(load_kernel, kv_heads),
        out_shape=(
            pltpu.VMEM((kv_heads, rows, depth), keys.dtype),
            pltpu.VMEM((kv_heads, rows, 2 * depth), values.dtype),
        ),
        in_specs=[anywhere] * 2,
        out_specs=(vmem,) * 2,
        scratch_shapes=[
            pltpu.VMEM(keys.shape, keys.dtype),
            pltpu.VMEM(values.shape, values.dtype),
            wide_scratch(2),
            pltpu.SemaphoreType.DMA((2,)),
        ],
        compiler_params=params,
        cost_estimate=pl.CostEstimate(flops=work * depth * 400, bytes_accessed=heads * rows * depth * 200, transcendentals=work),
    )(*[in_hbm(x) for x in (keys, values)])
    top, sums = pl.pallas_call(
        functools.partial(first_kernel, "ctx", pair, kv_heads, factor),
        out_shape=(top_shape, sums_shape),
        in_specs=[vmem] * (3 + len(near)),
        out_specs=(vmem,) * 2,
        scratch_shapes=[wide_scratch(2), keys_scratch, values_scratch],
        compiler_params=params,
        cost_estimate=pl.CostEstimate(flops=work * depth * 400, bytes_accessed=heads * rows * depth * 200, transcendentals=work),
    )(*[in_vmem(x) for x in (q_vmem, own_keys, own_values, *near)])

    out = None
    for hop in range(1, chips):
        last = hop == chips - 1
        if not last:
            far.append(far_pair(hop + 1))
        all_keys, all_values = far[hop - 1]
        first_keys, top = lax.optimization_barrier((all_keys[0], top))
        all_keys = [first_keys]
        if pair == 2:
            all_keys.append(lax.ppermute(first_keys, "ctx", swap))
            if not DIRECT:
                all_keys[1], first_values = lax.optimization_barrier((all_keys[1], all_values[0]))
                all_values = [first_values, lax.ppermute(first_values, "ctx", swap)]
        held = [] if out is None else [in_hbm(out)]
        weights, drop, out, *new_top = pl.pallas_call(
            functools.partial(keys_kernel, "ctx", pair, kv_heads, factor, hop, last),
            out_shape=(weights_shape, top_shape, out_shape) + (() if last else (top_shape,)),
            in_specs=[vmem] * (3 + pair) + [anywhere] * len(held),
            out_specs=(vmem, vmem, anywhere) + (() if last else (vmem,)),
            scratch_shapes=[wide_scratch(pair), parts_scratch, *out_scratch],
            input_output_aliases={3 + pair: 2} if held else {},
            compiler_params=params,
            cost_estimate=cost,
        )(
            in_vmem(q_vmem),
            *[in_vmem(x) for x in all_keys],
            in_vmem(top),
            in_vmem(sums),
            *held,
        )
        top = top if last else new_top[0]
        sums, out = pl.pallas_call(
            functools.partial(values_kernel, "ctx", pair, kv_heads, hop, last),
            out_shape=(sums_shape, out_shape),
            in_specs=[vmem] * (3 + pair) + [anywhere],
            out_specs=(vmem, anywhere),
            scratch_shapes=[wide_scratch(pair), values_scratch, *out_scratch],
            input_output_aliases={2 + pair: 0, 3 + pair: 1},
            compiler_params=params,
            cost_estimate=cost,
        )(
            *[in_vmem(x) for x in all_values],
            *[in_vmem(x) for x in (weights, drop, sums)],
            in_hbm(out),
        )
    return out


def solution(mesh):
    return jax.shard_map(
        functools.partial(local, mesh.shape["ctx"]),
        mesh=mesh,
        in_specs=(
            P(("seq", "ctx"), "head", None),
            P(("seq", "ctx"), "head", None),
            P(("seq", "ctx"), "head", None),
        ),
        out_specs=P(("seq", "ctx"), "head", None),
        check_vma=False,
    )
```

```python
import functools
import math

import jax
import jax.numpy as jnp
from jax import lax
from jax.experimental import pallas as pl
from jax.experimental.pallas import tpu as pltpu
from jax.sharding import PartitionSpec as P

VMEM_LIMIT = 30 * 1024 * 1024
TILE_ROWS = 512
NEG = -1e30


def tile_plan(rows, group):
    return math.gcd(rows, max(1, TILE_ROWS // group))


def split_into(packed, kv_heads, base, wide_ref, block_ref):
    total, depth = packed.shape
    count = total // kv_heads
    if kv_heads == 1:
        block_ref[0, base : base + count, :depth] = packed
        return
    wide_ref[...] = packed.astype(jnp.float32)
    for head in range(kv_heads):
        block = wide_ref[pl.ds(head, count, stride=kv_heads), :]
        block_ref[head, base : base + count, :depth] = block.astype(packed.dtype)


def split_keys(packed, kv_heads, factor, base, wide_ref, keys_ref):
    total, depth = packed.shape
    count = total // kv_heads
    wide_ref[...] = packed.astype(jnp.float32) * factor
    for head in range(kv_heads):
        block = wide_ref[pl.ds(head, count, stride=kv_heads), :]
        high = block.astype(packed.dtype)
        keys_ref[head, base : base + count, :depth] = high
        keys_ref[head, base : base + count, depth:] = (
            block - high.astype(jnp.float32)
        ).astype(packed.dtype)


def fill_ones(values_ref, depth):
    shape = (values_ref.shape[0], values_ref.shape[1], values_ref.shape[2] - depth)
    values_ref[:, :, depth:] = jnp.ones(shape, values_ref.dtype)


def tile_queries(q_ref, head, group, tile, positions):
    rows = q_ref[tile * positions : (tile + 1) * positions, head * group : (head + 1) * group, :]
    return rows.reshape(positions * group, q_ref.shape[2])


def scores_of(q_rows, keys):
    return lax.dot_general(
        q_rows, keys, (((1,), (1,)), ((), ())), preferred_element_type=jnp.float32
    )


def put_result(stage_ref, head, group, tile, positions, numer, total):
    result = (numer * (1.0 / total)).astype(stage_ref.dtype)
    stage_ref[tile * positions : (tile + 1) * positions, head * group : (head + 1) * group, :] = (
        result.reshape(positions, group, numer.shape[1])
    )


def out_copy(stage_ref, out_ref, sems, tile, positions):
    where = pl.ds(tile * positions, positions)
    return pltpu.make_async_copy(stage_ref.at[where], out_ref.at[where], sems.at[tile])


def load_kernel(kv_heads, *refs):
    k_hbm, v_hbm, keys_ref, values_ref, own_k, own_v, wide_ref, sems = refs
    copies = [
        pltpu.make_async_copy(source, target, sems.at[i])
        for i, (source, target) in enumerate(((k_hbm, own_k), (v_hbm, own_v)))
    ]
    for copy in copies:
        copy.start()
    fill_ones(values_ref, keys_ref.shape[2])
    copies[0].wait()
    split_into(own_k[...], kv_heads, 0, wide_ref.at[0], keys_ref)
    copies[1].wait()
    split_into(own_v[...], kv_heads, 0, wide_ref.at[1], values_ref)


def first_kernel(axis, pair, kv_heads, factor, *refs):
    q_ref, own_keys_ref, own_values_ref = refs[:3]
    near_refs = refs[3 : 1 + 2 * pair]
    top_ref, sums_ref = refs[1 + 2 * pair : 3 + 2 * pair]
    wide_ref, keys_ref, values_ref = refs[3 + 2 * pair :]
    rows, heads, depth = q_ref.shape
    group = heads // kv_heads
    positions = tile_plan(rows, group)
    tile_rows = positions * group
    tiles = rows // positions
    lane = lax.rem(lax.axis_index(axis), pair)

    keys_ref[:, :rows, :] = own_keys_ref[...]
    values_ref[:, :rows, :] = own_values_ref[...]
    if pair > 1:
        fill_ones(values_ref.at[:, rows:], depth)
        split_into(near_refs[0][...], kv_heads, rows, wide_ref.at[0], keys_ref)
        split_into(near_refs[1][...], kv_heads, rows, wide_ref.at[1], values_ref)
    bias = jnp.where(lane > 0, 0.0, NEG).astype(jnp.float32)

    for tile in range(tiles):
        for head in range(kv_heads):
            where = slice(tile * tile_rows, (tile + 1) * tile_rows)
            q_rows = tile_queries(q_ref, head, group, tile, positions)
            scores = scores_of(q_rows, keys_ref[head])
            own = scores[:, :rows].reshape(positions, group, rows)
            place = tile * positions + lax.broadcasted_iota(jnp.int32, own.shape, 0)
            own = jnp.where(lax.broadcasted_iota(jnp.int32, own.shape, 2) <= place, own, NEG)
            own = own.reshape(tile_rows, rows)
            if pair > 1:
                scores = jnp.concatenate([own, scores[:, rows:] + bias], axis=1)
            else:
                scores = own
            top = jnp.max(scores, axis=1, keepdims=True)
            weights = jnp.exp2((scores - top) * factor).astype(values_ref.dtype)
            top_ref[head, where, :] = jnp.broadcast_to(top * factor, (tile_rows, depth))
            sums_ref[head, where, :] = jnp.dot(
                weights, values_ref[head], preferred_element_type=jnp.float32
            )


def write_kernel(axis, pair, kv_heads, hop, *refs):
    sums_ref, out_ref, stage_ref, out_sems = refs[0], *refs[-3:]
    rows, heads, depth = stage_ref.shape
    group = heads // kv_heads
    positions = tile_plan(rows, group)
    tile_rows = positions * group
    tiles = rows // positions

    @pl.when(lax.div(lax.axis_index(axis), pair) == hop - 1)
    def _():
        for tile in range(tiles):
            where = slice(tile * tile_rows, (tile + 1) * tile_rows)
            for head in range(kv_heads):
                put_result(
                    stage_ref, head, group, tile, positions,
                    sums_ref[head, where, :depth], sums_ref[head, where, depth:],
                )
            out_copy(stage_ref, out_ref, out_sems, tile, positions).start()
        for tile in range(tiles):
            out_copy(stage_ref, out_ref, out_sems, tile, positions).wait()


def keys_kernel(axis, pair, kv_heads, factor, hop, last, *refs):
    q_ref = refs[0]
    key_refs = refs[1 : 1 + pair]
    old_ref, weights_ref, drop_ref = refs[1 + pair : 4 + pair]
    top_ref = None if last else refs[4 + pair]
    wide_ref, keys_ref = refs[-2:]
    rows, heads, depth = q_ref.shape
    group = heads // kv_heads
    positions = tile_plan(rows, group)
    tile_rows = positions * group
    tiles = rows // positions
    chip = lax.div(lax.axis_index(axis), pair)

    @pl.when(chip >= hop)
    def _():
        for block in range(pair):
            split_keys(
                key_refs[block][...], kv_heads, factor, block * rows, wide_ref.at[block], keys_ref
            )
        for tile in range(tiles):
            where = slice(tile * tile_rows, (tile + 1) * tile_rows)
            for head in range(kv_heads):
                q_rows = tile_queries(q_ref, head, group, tile, positions)
                scores = scores_of(jnp.concatenate([q_rows, q_rows], axis=1), keys_ref[head])
                old = old_ref[head, where, :]
                top = jnp.maximum(jnp.max(scores, axis=1, keepdims=True), old)
                if top_ref is not None:
                    top_ref[head, where, :] = top
                drop_ref[head, where, :] = old - top
                for part in range(pair * rows // depth):
                    weights_ref[head, part, where, :] = jnp.exp2(
                        scores[:, part * depth : (part + 1) * depth] - top
                    ).astype(weights_ref.dtype)


def values_kernel(axis, pair, kv_heads, hop, last, *refs):
    value_refs = refs[:pair]
    weights_ref, drop_ref, old_ref = refs[pair : 3 + pair]
    sums_ref, out_ref = refs[4 + pair : 6 + pair]
    wide_ref, values_ref, stage_ref, out_sems = refs[6 + pair :]
    rows, heads, depth = stage_ref.shape
    group = heads // kv_heads
    positions = tile_plan(rows, group)
    tile_rows = positions * group
    tiles = rows // positions
    chip = lax.div(lax.axis_index(axis), pair)

    def merged(head, tile):
        where = slice(tile * tile_rows, (tile + 1) * tile_rows)
        weights = jnp.concatenate(
            [weights_ref[head, part, where, :] for part in range(pair * rows // depth)], axis=1
        )
        sums = jnp.dot(weights, values_ref[head], preferred_element_type=jnp.float32)
        rescale = jnp.exp2(drop_ref[head, where, :])
        return (
            old_ref[head, where, :depth] * rescale + sums[:, :depth],
            old_ref[head, where, depth:] * rescale + sums[:, depth:],
        )

    @pl.when(chip >= hop)
    def _():
        fill_ones(values_ref, depth)
        for block in range(pair):
            split_into(value_refs[block][...], kv_heads, block * rows, wide_ref.at[block], values_ref)
        for tile in range(tiles):
            where = slice(tile * tile_rows, (tile + 1) * tile_rows)
            for head in range(kv_heads):
                numer, total = merged(head, tile)
                if last:
                    put_result(stage_ref, head, group, tile, positions, numer, total)
                else:
                    sums_ref[head, where, :depth] = numer
                    sums_ref[head, where, depth:] = total
            if last:
                out_copy(stage_ref, out_ref, out_sems, tile, positions).start()
        if last:
            for tile in range(tiles):
                out_copy(stage_ref, out_ref, out_sems, tile, positions).wait()


def in_vmem(array):
    return pltpu.with_memory_space_constraint(array, pltpu.VMEM)


def in_hbm(array):
    return pltpu.with_memory_space_constraint(array, pltpu.HBM)


def local(ctx_size, queries, keys, values):
    rows, heads, depth = queries.shape
    kv_heads = keys.shape[1]
    group = heads // kv_heads
    pair = 2 if ctx_size % 2 == 0 else 1
    chips = ctx_size // pair
    factor = math.log2(math.e) / math.sqrt(depth)
    vmem = pl.BlockSpec(memory_space=pltpu.VMEM)
    anywhere = pl.BlockSpec(memory_space=pl.ANY)

    raw_keys, raw_values = keys, values
    keys = keys.reshape(rows * kv_heads, depth)
    values = values.reshape(rows * kv_heads, depth)
    swap = [(i, i ^ 1) for i in range(ctx_size)]

    def across(array, hop, cross):
        route = [
            (i, (i // pair + hop) % chips * pair + (i % pair ^ cross)) for i in range(ctx_size)
        ]
        return lax.ppermute(array, "ctx", route).reshape(rows * kv_heads, depth)

    def far_pair(hop):
        far_keys = [across(raw_keys, hop, pair - 1)]
        far_values = [across(values, hop, pair - 1)]
        return far_keys, far_values

    far = [far_pair(1)]
    near = []
    if pair == 2:
        near_values = lax.ppermute(raw_values, "ctx", swap).reshape(rows * kv_heads, depth)
        near = [lax.ppermute(keys, "ctx", swap), near_values]

    positions = tile_plan(rows, group)
    tiles = rows // positions
    work = heads * rows * rows * pair
    cost = pl.CostEstimate(
        flops=work * depth * 4, bytes_accessed=heads * rows * depth * 2, transcendentals=work
    )

    def wide_scratch(count):
        return pltpu.VMEM((count, *keys.shape), jnp.float32)

    keys_scratch = pltpu.VMEM((kv_heads, pair * rows, depth), keys.dtype)
    parts_scratch = pltpu.VMEM((kv_heads, pair * rows, 2 * depth), keys.dtype)
    values_scratch = pltpu.VMEM((kv_heads, pair * rows, 2 * depth), keys.dtype)
    out_scratch = [pltpu.VMEM(queries.shape, queries.dtype), pltpu.SemaphoreType.DMA((tiles,))]
    params = pltpu.CompilerParams(vmem_limit_bytes=VMEM_LIMIT)
    out_shape = jax.ShapeDtypeStruct(queries.shape, queries.dtype)
    top_shape = pltpu.VMEM((kv_heads, rows * group, depth), jnp.float32)
    sums_shape = pltpu.VMEM((kv_heads, rows * group, 2 * depth), jnp.float32)
    weights_shape = pltpu.VMEM(
        (kv_heads, pair * rows // depth, rows * group, depth), values.dtype
    )
    q_vmem = queries
    own_keys, own_values = pl.pallas_call(
        functools.partial(load_kernel, kv_heads),
        out_shape=(
            pltpu.VMEM((kv_heads, rows, depth), keys.dtype),
            pltpu.VMEM((kv_heads, rows, 2 * depth), values.dtype),
        ),
        in_specs=[anywhere] * 2,
        out_specs=(vmem,) * 2,
        scratch_shapes=[
            pltpu.VMEM(keys.shape, keys.dtype),
            pltpu.VMEM(values.shape, values.dtype),
            wide_scratch(2),
            pltpu.SemaphoreType.DMA((2,)),
        ],
        compiler_params=params,
        cost_estimate=pl.CostEstimate(flops=work * depth * 400, bytes_accessed=heads * rows * depth * 200, transcendentals=work),
    )(*[in_hbm(x) for x in (keys, values)])
    top, sums = pl.pallas_call(
        functools.partial(first_kernel, "ctx", pair, kv_heads, factor),
        out_shape=(top_shape, sums_shape),
        in_specs=[vmem] * (3 + len(near)),
        out_specs=(vmem,) * 2,
        scratch_shapes=[wide_scratch(2), keys_scratch, values_scratch],
        compiler_params=params,
        cost_estimate=pl.CostEstimate(flops=work * depth * 400, bytes_accessed=heads * rows * depth * 200, transcendentals=work),
    )(*[in_vmem(x) for x in (q_vmem, own_keys, own_values, *near)])

    out = None
    for hop in range(1, chips):
        last = hop == chips - 1
        if not last:
            far.append(far_pair(hop + 1))
        all_keys, all_values = far[hop - 1]
        held = [] if out is None else [in_hbm(out)]
        out = pl.pallas_call(
            functools.partial(write_kernel, "ctx", pair, kv_heads, hop),
            out_shape=out_shape,
            in_specs=[vmem] + [anywhere] * len(held),
            out_specs=anywhere,
            scratch_shapes=out_scratch,
            input_output_aliases={1: 0} if held else {},
            compiler_params=params,
            cost_estimate=cost,
        )(in_vmem(sums), *held)
        first_keys, top, out = lax.optimization_barrier((all_keys[0], top, out))
        all_keys = [first_keys]
        if pair == 2:
            all_keys.append(lax.ppermute(first_keys, "ctx", swap))
            first_values, sums = lax.optimization_barrier((all_values[0], sums))
            all_values = [first_values, lax.ppermute(first_values, "ctx", swap)]
        weights, drop, *new_top = pl.pallas_call(
            functools.partial(keys_kernel, "ctx", pair, kv_heads, factor, hop, last),
            out_shape=(weights_shape, top_shape) + (() if last else (top_shape,)),
            in_specs=[vmem] * (2 + pair),
            out_specs=(vmem, vmem) + (() if last else (vmem,)),
            scratch_shapes=[wide_scratch(pair), parts_scratch],
            compiler_params=params,
            cost_estimate=cost,
        )(*[in_vmem(x) for x in (q_vmem, *all_keys, top)])
        top = top if last else new_top[0]
        sums, out = pl.pallas_call(
            functools.partial(values_kernel, "ctx", pair, kv_heads, hop, last),
            out_shape=(sums_shape, out_shape),
            in_specs=[vmem] * (3 + pair) + [anywhere],
            out_specs=(vmem, anywhere),
            scratch_shapes=[wide_scratch(pair), values_scratch, *out_scratch],
            input_output_aliases={2 + pair: 0, 3 + pair: 1},
            compiler_params=params,
            cost_estimate=cost,
        )(
            *[in_vmem(x) for x in all_values],
            *[in_vmem(x) for x in (weights, drop, sums)],
            in_hbm(out),
        )
    return out


def solution(mesh):
    return jax.shard_map(
        functools.partial(local, mesh.shape["ctx"]),
        mesh=mesh,
        in_specs=(
            P(("seq", "ctx"), "head", None),
            P(("seq", "ctx"), "head", None),
            P(("seq", "ctx"), "head", None),
        ),
        out_specs=P(("seq", "ctx"), "head", None),
        check_vma=False,
    )
```

```python
import functools
import math

import jax
import jax.numpy as jnp
from jax import lax
from jax.experimental import pallas as pl
from jax.experimental.pallas import tpu as pltpu
from jax.sharding import PartitionSpec as P

VMEM_LIMIT = 30 * 1024 * 1024
TILE_ROWS = 512
NEG = -1e30


def tile_plan(rows, group):
    return math.gcd(rows, max(1, TILE_ROWS // group))


def split_into(packed, kv_heads, base, wide_ref, block_ref):
    total, depth = packed.shape
    count = total // kv_heads
    if kv_heads == 1:
        block_ref[0, base : base + count, :depth] = packed
        return
    wide_ref[...] = packed.astype(jnp.float32)
    for head in range(kv_heads):
        block = wide_ref[pl.ds(head, count, stride=kv_heads), :]
        block_ref[head, base : base + count, :depth] = block.astype(packed.dtype)


def split_keys(packed, kv_heads, factor, base, wide_ref, keys_ref):
    total, depth = packed.shape
    count = total // kv_heads
    wide_ref[...] = packed.astype(jnp.float32) * factor
    for head in range(kv_heads):
        block = wide_ref[pl.ds(head, count, stride=kv_heads), :]
        high = block.astype(packed.dtype)
        keys_ref[head, base : base + count, :depth] = high
        keys_ref[head, base : base + count, depth:] = (
            block - high.astype(jnp.float32)
        ).astype(packed.dtype)


def fill_ones(values_ref, depth):
    shape = (values_ref.shape[0], values_ref.shape[1], values_ref.shape[2] - depth)
    values_ref[:, :, depth:] = jnp.ones(shape, values_ref.dtype)


def tile_queries(q_ref, head, group, tile, positions):
    rows = q_ref[tile * positions : (tile + 1) * positions, head * group : (head + 1) * group, :]
    return rows.reshape(positions * group, q_ref.shape[2])


def scores_of(q_rows, keys):
    return lax.dot_general(
        q_rows, keys, (((1,), (1,)), ((), ())), preferred_element_type=jnp.float32
    )


def put_result(stage_ref, head, group, tile, positions, numer, total):
    result = (numer * (1.0 / total)).astype(stage_ref.dtype)
    stage_ref[tile * positions : (tile + 1) * positions, head * group : (head + 1) * group, :] = (
        result.reshape(positions, group, numer.shape[1])
    )


def out_copy(stage_ref, out_ref, sems, tile, positions):
    where = pl.ds(tile * positions, positions)
    return pltpu.make_async_copy(stage_ref.at[where], out_ref.at[where], sems.at[tile])


def load_kernel(kv_heads, *refs):
    k_hbm, v_hbm, keys_ref, values_ref, own_k, own_v, wide_ref, sems = refs
    copies = [
        pltpu.make_async_copy(source, target, sems.at[i])
        for i, (source, target) in enumerate(((k_hbm, own_k), (v_hbm, own_v)))
    ]
    for copy in copies:
        copy.start()
    fill_ones(values_ref, keys_ref.shape[2])
    copies[0].wait()
    split_into(own_k[...], kv_heads, 0, wide_ref.at[0], keys_ref)
    copies[1].wait()
    split_into(own_v[...], kv_heads, 0, wide_ref.at[1], values_ref)


def first_kernel(axis, pair, kv_heads, factor, *refs):
    q_ref, own_keys_ref, own_values_ref = refs[:3]
    near_refs = refs[3 : 1 + 2 * pair]
    top_ref, sums_ref = refs[1 + 2 * pair : 3 + 2 * pair]
    wide_ref, keys_ref, values_ref = refs[3 + 2 * pair :]
    rows, heads, depth = q_ref.shape
    group = heads // kv_heads
    positions = tile_plan(rows, group)
    tile_rows = positions * group
    tiles = rows // positions
    lane = lax.rem(lax.axis_index(axis), pair)

    keys_ref[:, :rows, :] = own_keys_ref[...]
    values_ref[:, :rows, :] = own_values_ref[...]
    if pair > 1:
        fill_ones(values_ref.at[:, rows:], depth)
        split_into(near_refs[0][...], kv_heads, rows, wide_ref.at[0], keys_ref)
        split_into(near_refs[1][...], kv_heads, rows, wide_ref.at[1], values_ref)
    bias = jnp.where(lane > 0, 0.0, NEG).astype(jnp.float32)

    for tile in range(tiles):
        for head in range(kv_heads):
            where = slice(tile * tile_rows, (tile + 1) * tile_rows)
            q_rows = tile_queries(q_ref, head, group, tile, positions)
            scores = scores_of(q_rows, keys_ref[head])
            own = scores[:, :rows].reshape(positions, group, rows)
            place = tile * positions + lax.broadcasted_iota(jnp.int32, own.shape, 0)
            own = jnp.where(lax.broadcasted_iota(jnp.int32, own.shape, 2) <= place, own, NEG)
            own = own.reshape(tile_rows, rows)
            if pair > 1:
                scores = jnp.concatenate([own, scores[:, rows:] + bias], axis=1)
            else:
                scores = own
            top = jnp.max(scores, axis=1, keepdims=True)
            weights = jnp.exp2((scores - top) * factor).astype(values_ref.dtype)
            top_ref[head, where, :] = jnp.broadcast_to(top * factor, (tile_rows, depth))
            sums_ref[head, where, :] = jnp.dot(
                weights, values_ref[head], preferred_element_type=jnp.float32
            )


def write_kernel(axis, pair, kv_heads, hop, *refs):
    sums_ref, out_ref, stage_ref, out_sems = refs[0], *refs[-3:]
    rows, heads, depth = stage_ref.shape
    group = heads // kv_heads
    positions = tile_plan(rows, group)
    tile_rows = positions * group
    tiles = rows // positions

    @pl.when(lax.div(lax.axis_index(axis), pair) == hop - 1)
    def _():
        for tile in range(tiles):
            where = slice(tile * tile_rows, (tile + 1) * tile_rows)
            for head in range(kv_heads):
                put_result(
                    stage_ref, head, group, tile, positions,
                    sums_ref[head, where, :depth], sums_ref[head, where, depth:],
                )
            out_copy(stage_ref, out_ref, out_sems, tile, positions).start()
        for tile in range(tiles):
            out_copy(stage_ref, out_ref, out_sems, tile, positions).wait()


def early_kernel(axis, pair, kv_heads, factor, hop, *refs):
    q_ref, key_ref, old_ref, scores_ref, top_ref, wide_ref, keys_ref = refs
    rows, heads, depth = q_ref.shape
    group = heads // kv_heads
    positions = tile_plan(rows, group)
    tile_rows = positions * group
    tiles = rows // positions

    @pl.when(lax.div(lax.axis_index(axis), pair) >= hop)
    def _():
        split_keys(key_ref[...], kv_heads, factor, 0, wide_ref.at[0], keys_ref)
        for tile in range(tiles):
            where = slice(tile * tile_rows, (tile + 1) * tile_rows)
            for head in range(kv_heads):
                q_rows = tile_queries(q_ref, head, group, tile, positions)
                scores = scores_of(jnp.concatenate([q_rows, q_rows], axis=1), keys_ref[head])
                scores_ref[head, where, :] = scores
                top_ref[head, where, :] = jnp.maximum(
                    jnp.max(scores, axis=1, keepdims=True), old_ref[head, where, :]
                )


def keys_kernel(axis, pair, kv_heads, factor, hop, last, *refs):
    q_ref, old_ref, early_ref, early_top_ref = refs[:4]
    key_refs = refs[4 : 3 + pair]
    weights_ref, drop_ref = refs[3 + pair : 5 + pair]
    top_ref = None if last else refs[5 + pair]
    wide_ref, keys_ref = refs[-2:]
    rows, heads, depth = q_ref.shape
    group = heads // kv_heads
    positions = tile_plan(rows, group)
    tile_rows = positions * group
    tiles = rows // positions
    chip = lax.div(lax.axis_index(axis), pair)

    @pl.when(chip >= hop)
    def _():
        for at, key_ref in enumerate(key_refs):
            split_keys(key_ref[...], kv_heads, factor, at * rows, wide_ref.at[at], keys_ref)
        for tile in range(tiles):
            where = slice(tile * tile_rows, (tile + 1) * tile_rows)
            for head in range(kv_heads):
                scores = [early_ref[head, where, :]]
                top = early_top_ref[head, where, :]
                if key_refs:
                    q_rows = tile_queries(q_ref, head, group, tile, positions)
                    scores.append(
                        scores_of(jnp.concatenate([q_rows, q_rows], axis=1), keys_ref[head])
                    )
                    top = jnp.maximum(jnp.max(scores[1], axis=1, keepdims=True), top)
                if top_ref is not None:
                    top_ref[head, where, :] = top
                drop_ref[head, where, :] = old_ref[head, where, :] - top
                part = 0
                for piece in scores:
                    for at in range(0, piece.shape[1], depth):
                        weights_ref[head, part, where, :] = jnp.exp2(
                            piece[:, at : at + depth] - top
                        ).astype(weights_ref.dtype)
                        part += 1


def values_kernel(axis, pair, kv_heads, hop, last, *refs):
    value_refs = refs[:pair]
    weights_ref, drop_ref, old_ref = refs[pair : 3 + pair]
    sums_ref, out_ref = refs[4 + pair : 6 + pair]
    wide_ref, values_ref, stage_ref, out_sems = refs[6 + pair :]
    rows, heads, depth = stage_ref.shape
    group = heads // kv_heads
    positions = tile_plan(rows, group)
    tile_rows = positions * group
    tiles = rows // positions
    chip = lax.div(lax.axis_index(axis), pair)

    def merged(head, tile):
        where = slice(tile * tile_rows, (tile + 1) * tile_rows)
        weights = jnp.concatenate(
            [weights_ref[head, part, where, :] for part in range(pair * rows // depth)], axis=1
        )
        sums = jnp.dot(weights, values_ref[head], preferred_element_type=jnp.float32)
        rescale = jnp.exp2(drop_ref[head, where, :])
        return (
            old_ref[head, where, :depth] * rescale + sums[:, :depth],
            old_ref[head, where, depth:] * rescale + sums[:, depth:],
        )

    @pl.when(chip >= hop)
    def _():
        fill_ones(values_ref, depth)
        for block in range(pair):
            split_into(value_refs[block][...], kv_heads, block * rows, wide_ref.at[block], values_ref)
        for tile in range(tiles):
            where = slice(tile * tile_rows, (tile + 1) * tile_rows)
            for head in range(kv_heads):
                numer, total = merged(head, tile)
                if last:
                    put_result(stage_ref, head, group, tile, positions, numer, total)
                else:
                    sums_ref[head, where, :depth] = numer
                    sums_ref[head, where, depth:] = total
            if last:
                out_copy(stage_ref, out_ref, out_sems, tile, positions).start()
        if last:
            for tile in range(tiles):
                out_copy(stage_ref, out_ref, out_sems, tile, positions).wait()


def in_vmem(array):
    return pltpu.with_memory_space_constraint(array, pltpu.VMEM)


def in_hbm(array):
    return pltpu.with_memory_space_constraint(array, pltpu.HBM)


def local(ctx_size, queries, keys, values):
    rows, heads, depth = queries.shape
    kv_heads = keys.shape[1]
    group = heads // kv_heads
    pair = 2 if ctx_size % 2 == 0 else 1
    chips = ctx_size // pair
    factor = math.log2(math.e) / math.sqrt(depth)
    vmem = pl.BlockSpec(memory_space=pltpu.VMEM)
    anywhere = pl.BlockSpec(memory_space=pl.ANY)

    raw_keys, raw_values = keys, values
    keys = keys.reshape(rows * kv_heads, depth)
    values = values.reshape(rows * kv_heads, depth)
    swap = [(i, i ^ 1) for i in range(ctx_size)]

    def across(array, hop, cross):
        route = [
            (i, (i // pair + hop) % chips * pair + (i % pair ^ cross)) for i in range(ctx_size)
        ]
        return lax.ppermute(array, "ctx", route).reshape(rows * kv_heads, depth)

    def far_pair(hop):
        far_keys = [across(raw_keys, hop, pair - 1)]
        far_values = [across(values, hop, pair - 1)]
        return far_keys, far_values

    far = [far_pair(1)]
    near = []
    if pair == 2:
        near_values = lax.ppermute(raw_values, "ctx", swap).reshape(rows * kv_heads, depth)
        near = [lax.ppermute(keys, "ctx", swap), near_values]

    positions = tile_plan(rows, group)
    tiles = rows // positions
    work = heads * rows * rows * pair
    cost = pl.CostEstimate(
        flops=work * depth * 4, bytes_accessed=heads * rows * depth * 2, transcendentals=work
    )

    def wide_scratch(count):
        return pltpu.VMEM((count, *keys.shape), jnp.float32)

    keys_scratch = pltpu.VMEM((kv_heads, pair * rows, depth), keys.dtype)
    early_scratch = pltpu.VMEM((kv_heads, rows, 2 * depth), keys.dtype)
    early_shape = pltpu.VMEM((kv_heads, rows * group, rows), jnp.float32)
    values_scratch = pltpu.VMEM((kv_heads, pair * rows, 2 * depth), keys.dtype)
    out_scratch = [pltpu.VMEM(queries.shape, queries.dtype), pltpu.SemaphoreType.DMA((tiles,))]
    params = pltpu.CompilerParams(vmem_limit_bytes=VMEM_LIMIT)
    out_shape = jax.ShapeDtypeStruct(queries.shape, queries.dtype)
    top_shape = pltpu.VMEM((kv_heads, rows * group, depth), jnp.float32)
    sums_shape = pltpu.VMEM((kv_heads, rows * group, 2 * depth), jnp.float32)
    weights_shape = pltpu.VMEM(
        (kv_heads, pair * rows // depth, rows * group, depth), values.dtype
    )
    q_vmem = queries
    own_keys, own_values = pl.pallas_call(
        functools.partial(load_kernel, kv_heads),
        out_shape=(
            pltpu.VMEM((kv_heads, rows, depth), keys.dtype),
            pltpu.VMEM((kv_heads, rows, 2 * depth), values.dtype),
        ),
        in_specs=[anywhere] * 2,
        out_specs=(vmem,) * 2,
        scratch_shapes=[
            pltpu.VMEM(keys.shape, keys.dtype),
            pltpu.VMEM(values.shape, values.dtype),
            wide_scratch(2),
            pltpu.SemaphoreType.DMA((2,)),
        ],
        compiler_params=params,
        cost_estimate=pl.CostEstimate(flops=work * depth * 400, bytes_accessed=heads * rows * depth * 200, transcendentals=work),
    )(*[in_hbm(x) for x in (keys, values)])
    top, sums = pl.pallas_call(
        functools.partial(first_kernel, "ctx", pair, kv_heads, factor),
        out_shape=(top_shape, sums_shape),
        in_specs=[vmem] * (3 + len(near)),
        out_specs=(vmem,) * 2,
        scratch_shapes=[wide_scratch(2), keys_scratch, values_scratch],
        compiler_params=params,
        cost_estimate=pl.CostEstimate(flops=work * depth * 400, bytes_accessed=heads * rows * depth * 200, transcendentals=work),
    )(*[in_vmem(x) for x in (q_vmem, own_keys, own_values, *near)])

    out = None
    for hop in range(1, chips):
        last = hop == chips - 1
        if not last:
            far.append(far_pair(hop + 1))
        all_keys, all_values = far[hop - 1]
        held = [] if out is None else [in_hbm(out)]
        out = pl.pallas_call(
            functools.partial(write_kernel, "ctx", pair, kv_heads, hop),
            out_shape=out_shape,
            in_specs=[vmem] + [anywhere] * len(held),
            out_specs=anywhere,
            scratch_shapes=out_scratch,
            input_output_aliases={1: 0} if held else {},
            compiler_params=params,
            cost_estimate=cost,
        )(in_vmem(sums), *held)
        first_keys, top, out = lax.optimization_barrier((all_keys[0], top, out))
        all_keys = [first_keys]
        early, early_top = pl.pallas_call(
            functools.partial(early_kernel, "ctx", pair, kv_heads, factor, hop),
            out_shape=(early_shape, top_shape),
            in_specs=[vmem] * 3,
            out_specs=(vmem,) * 2,
            scratch_shapes=[wide_scratch(1), early_scratch],
            compiler_params=params,
            cost_estimate=cost,
        )(*[in_vmem(x) for x in (q_vmem, all_keys[0], top)])
        if pair == 2:
            all_keys.append(lax.ppermute(first_keys, "ctx", swap))
            first_values, early_top = lax.optimization_barrier((all_values[0], early_top))
            all_values = [first_values, lax.ppermute(first_values, "ctx", swap)]
        weights, drop, *new_top = pl.pallas_call(
            functools.partial(keys_kernel, "ctx", pair, kv_heads, factor, hop, last),
            out_shape=(weights_shape, top_shape) + (() if last else (top_shape,)),
            in_specs=[vmem] * (3 + pair),
            out_specs=(vmem, vmem) + (() if last else (vmem,)),
            scratch_shapes=[wide_scratch(1), early_scratch],
            compiler_params=params,
            cost_estimate=cost,
        )(*[in_vmem(x) for x in (q_vmem, top, early, early_top, *all_keys[1:])])
        top = top if last else new_top[0]
        sums, out = pl.pallas_call(
            functools.partial(values_kernel, "ctx", pair, kv_heads, hop, last),
            out_shape=(sums_shape, out_shape),
            in_specs=[vmem] * (3 + pair) + [anywhere],
            out_specs=(vmem, anywhere),
            scratch_shapes=[wide_scratch(pair), values_scratch, *out_scratch],
            input_output_aliases={2 + pair: 0, 3 + pair: 1},
            compiler_params=params,
            cost_estimate=cost,
        )(
            *[in_vmem(x) for x in all_values],
            *[in_vmem(x) for x in (weights, drop, sums)],
            in_hbm(out),
        )
    return out


def solution(mesh):
    return jax.shard_map(
        functools.partial(local, mesh.shape["ctx"]),
        mesh=mesh,
        in_specs=(
            P(("seq", "ctx"), "head", None),
            P(("seq", "ctx"), "head", None),
            P(("seq", "ctx"), "head", None),
        ),
        out_specs=P(("seq", "ctx"), "head", None),
        check_vma=False,
    )
```
